32 devices in a mesh: valve: 4 (over y, core), bulk: 8 (over z, x).
Axes of the slice: x: 2, y: 2, z: 4, core: 2. Of those that a mesh axis runs over, the one named last changes fastest.
Arguments:
- solution: float32 [5, 64, 32768], P(None, None, ('valve', 'bulk')), may hold values from -6 to 6
- velocity: float32 [3, 32768], P(None, ('valve', 'bulk')), may hold values from -1 to 1
- inv_jacobian: float32 [64, 32768], P(None, ('valve', 'bulk')), may hold values from 0.5 to 3
- face_speed: float32 [96, 32768], P(None, ('valve', 'bulk')), may hold values from -6 to 6
- face_link: int32 [6, 32768], P(None, ('valve', 'bulk')), may hold values from 0 to 6271, as said below
- donor_elem: int32 [262144], P(('valve', 'bulk')), may hold values from 0 to 1023
- ref_coords: float32 [3, 262144], P(None, ('valve', 'bulk')), may hold values from -1 to 1
- owner_list: int32 [262144, 1], P(('valve', 'bulk')), may hold values from 0 to 7; in each aligned block of 8192 rows (0 to 8191, 8192 to 16383, ...) at most 2048 rows name the same one
Outputs:
- section_rate: float32 [5, 64, 32768], P(None, None, ('valve', 'bulk'))
- fringe_values: float32 [5, 524288], P(None, ('valve', 'bulk'))
The draws below stay inside these ranges and needn't reach their ends.
Inputs may be any that keep to these rules, and one draw needn't show every extreme that they name: `face_link`: on each device, the values 6 * 1024 to 6271 appear exactly once each; every other face slot links to another slot of the same device that links back to it. `owner_list`: among the receptors of one device no owner is named more than 2048 times; in every draw some device names some owner exactly 2048 times.
All inputs are finite; a program needn't handle non-finite values.
Results may differ from the reference program's by a relative error of at most 0.0003.
Values sent between devices are 32-bit elements; how exact they have to be, the bound alone decides.
A program may use at most 192 MiB of HBM per device.

```python
import math
import jax
import jax.numpy as jnp
import numpy as np
from jax import lax

NVAR = 5
SOLPTS = 64
FLXPTS = 96
E_DEV = 1024
IFACE = 64
REC_DEV = 8192
CAP = 2048
NEL = 32768
NREC = 262144
SLOTS = 524288
N_VALVE = 4
N_BULK = 8
DEVICES = 32


def draw_face_link(key, part):
    faces_total = 6 * E_DEV

    def one_device(device):
        order = jax.random.permutation(jax.random.fold_in(key, device), faces_total).astype(jnp.int32)
        places = jnp.arange(faces_total, dtype=jnp.int32)
        paired = 2 * IFACE + jnp.bitwise_xor(places - 2 * IFACE, 1)
        partner = jnp.take(order, jnp.clip(paired, 0, faces_total - 1))
        values = jnp.where(places < 2 * IFACE, faces_total + places, partner)
        return jnp.zeros((faces_total,), jnp.int32).at[order].set(values).reshape(6, E_DEV)
    stacked = jax.vmap(one_device)(jnp.arange(DEVICES, dtype=jnp.int32))
    return jnp.transpose(stacked, (1, 0, 2)).reshape(6, DEVICES * E_DEV)


def touch_ends(values, rng, low, largest):
    spot = [jax.random.randint(jax.random.fold_in(rng, axis), (), 0, length) for axis, length in enumerate(values.shape)]
    widest = values.shape.index(max(values.shape))
    beside = spot[:widest] + [(spot[widest] + 1) % values.shape[widest]] + spot[widest + 1:]
    return values.at[tuple(spot)].set(low).at[tuple(beside)].set(largest)


def level_of(rng, shape, shards, low, largest):
    gain = 1.0
    for dim, blocks in shards:
        steps = jax.random.uniform(jax.random.fold_in(jax.random.fold_in(rng, 6), dim), (blocks,), jnp.float32, low / len(shards), largest / len(shards))
        gain = gain * jnp.repeat(jnp.exp(steps), shape[dim] // blocks).reshape((-1,) + (1,) * (len(shape) - 1 - dim))
    return gain


def deal_out(own_key, own, number, rows, count, top, reach, skew):
    sequence = jax.random.permutation(own_key, count)
    heavy_load, ordinary = portions_of(count, rows * top, reach, skew, True), portions_of(count, rows * top, reach, skew, False)
    places = jnp.arange(count)

    def named(lengths, rotation):
        used = int((lengths > 0).sum())
        fixed = max(1, used // 4)
        shifted = fixed + (places - fixed + rotation * (used - fixed)) % max(1, count - fixed)
        return jnp.zeros((count,), jnp.int32).at[sequence[jnp.where(places < fixed, places, shifted)]].set(jnp.asarray(lengths, jnp.int32))

    lengths = jnp.where(number % 4 == 0, named(heavy_load, number // 4), named(ordinary, number - number // 4 - 1))
    mixed = jax.random.permutation(jax.random.fold_in(own, 3), count)
    donor, receiver = mixed[0:count // 2 * 2:2], mixed[1:count // 2 * 2:2]
    margin = jnp.minimum(lengths[donor] - 1, reach - lengths[receiver]) // 2
    margin = jnp.where((donor == sequence[0]) | (receiver == sequence[0]) | (lengths[receiver] == 0), 0, jnp.maximum(margin, 0))
    shifted = jax.random.randint(jax.random.fold_in(own, 4), (count // 2,), 0, 1 << 20) % (margin + 1)
    lengths = lengths.at[donor].add(-shifted).at[receiver].add(shifted)
    items = jnp.searchsorted(jnp.cumsum(lengths), jnp.arange(rows * top), side="right").astype(jnp.int32)
    grid = items.reshape(top, rows).T
    grid = grid[jax.random.permutation(jax.random.fold_in(own, 1), rows)]
    rotation = jax.random.randint(jax.random.fold_in(own, 2), (rows, 1), 0, top)
    return jnp.take_along_axis(grid, (jnp.arange(top)[None, :] + rotation) % top, axis=1)


def portions_of(amount, total, bound, lean, full):
    portions = [(1 << 20) // math.isqrt(standing ** lean) + 1 for standing in range(1, amount + 1)]
    largest = bound if full else min(bound, max(-(-total // amount), total * portions[0] // sum(portions)))
    least = 1 if total - largest >= amount - 1 else 0
    given, surplus = [largest] + [least] * (amount - 1), total - largest - least * (amount - 1)
    while surplus > 0:
        movable = [i for i in range(1, amount) if given[i] < largest] or [i for i in range(1, amount) if given[i] < bound]
        pool, budget = sum([portions[i] for i in movable]), surplus
        for i in movable:
            addition = min(bound - given[i], max(1, budget * portions[i] // pool), surplus)
            given[i] = given[i] + addition
            surplus = surplus - addition
    return np.array(given)


def scatter_about(key, dims, deviation, reach, shards=(), held_as=jnp.bfloat16):
    entries = deviation * jax.random.normal(key, dims, jnp.float32)
    if shards:
        entries = entries * level_of(key, dims, shards, -0.22, 0.18)
    return jnp.clip(entries, -reach, reach).astype(held_as)


def setup_inputs(seed: int = 0) -> dict:
    key_list = jax.random.split(jax.random.key(seed), 9)
    solution = scatter_about(key_list[0], (NVAR, SOLPTS, NEL), 1.0, 6.0, ((2, 32),), jnp.float32)
    velocity = jnp.clip(jax.random.uniform(key_list[1], (3, NEL), jnp.float32, -1.0, 1.0) * level_of(key_list[1], (3, NEL), ((1, 32),), -0.4, 0.0), -1.0, 1.0)
    inv_jacobian = jnp.clip(jnp.exp(math.log(3.0) - 1.7917595 * jax.random.uniform(key_list[2], (SOLPTS, NEL), jnp.float32) ** level_of(key_list[2], (SOLPTS, NEL), ((1, 32),), -0.2, 0.2)), 0.5, 3.0)
    face_speed = scatter_about(key_list[3], (FLXPTS, NEL), 1.0, 6.0, ((1, 32),), jnp.float32)
    face_link = draw_face_link(jax.random.fold_in(key_list[8], 71), 0)
    donor_elem = touch_ends(jax.random.randint(key_list[5], (NREC,), 0, E_DEV), jax.random.fold_in(key_list[5], 1), 0, E_DEV - 1).astype(jnp.int32)
    ref_coords = jnp.clip(jax.random.uniform(key_list[6], (3, NREC), jnp.float32, -1.0, 1.0) * level_of(key_list[6], (3, NREC), ((1, 32),), -0.4, 0.0), -1.0, 1.0)
    owner_list_keys = jax.random.split(jax.random.fold_in(key_list[7], 1), NREC // REC_DEV)
    owner_list_turns = jax.random.permutation(jax.random.fold_in(key_list[7], 3), NREC // REC_DEV)
    owner_list = jax.vmap(lambda own, number: deal_out(jax.random.fold_in(key_list[7], 2), own, number, REC_DEV, N_BULK, 1, CAP, 2))(owner_list_keys, owner_list_turns).reshape((NREC, 1))
    return dict(solution=solution, velocity=velocity, inv_jacobian=inv_jacobian, face_speed=face_speed, face_link=face_link, donor_elem=donor_elem, ref_coords=ref_coords, owner_list=owner_list)


gauss_nodes = (-0.8611363115940526, -0.3399810435848563, 0.3399810435848563, 0.8611363115940526)
quad_weights = (0.3478548451374538, 0.6521451548625461, 0.6521451548625461, 0.3478548451374538)
section_step = 0.2


def lagrange_at(x):
    values = []
    for j in range(4):
        factor = 1.0
        for m in range(4):
            if m != j:
                factor = factor * (x - gauss_nodes[m]) / (gauss_nodes[j] - gauss_nodes[m])
        values.append(factor)
    return values


def tables():
    slopes = np.zeros((4, 4))
    for i in range(4):
        for j in range(4):
            summed = 0.0
            for m in range(4):
                if m != j:
                    product = 1.0 / (gauss_nodes[j] - gauss_nodes[m])
                    for n in range(4):
                        if n != j and n != m:
                            product = product * (gauss_nodes[i] - gauss_nodes[n]) / (gauss_nodes[j] - gauss_nodes[n])
                    summed = summed + product
            slopes[i, j] = summed
    end_values = [lagrange_at(-1.0), lagrange_at(1.0)]
    extrapolate = np.zeros((96, 64))
    lifting = np.zeros((64, 96))
    derivative = np.zeros((3, 64, 64))
    for p in range(64):
        point_idx = (p // 16, (p // 4) % 4, p % 4)
        for f in range(6):
            normal_dir = f // 2
            across = [t for t in range(3) if t != normal_dir]
            q = point_idx[across[0]] * 4 + point_idx[across[1]]
            flux_row = q * 6 + f
            extrapolate[flux_row, p] = end_values[f % 2][point_idx[normal_dir]]
            lifting[p, flux_row] = end_values[f % 2][point_idx[normal_dir]] / quad_weights[point_idx[normal_dir]]
        for s in range(64):
            other_idx = (s // 16, (s // 4) % 4, s % 4)
            for normal_dir in range(3):
                if all(point_idx[t] == other_idx[t] for t in range(3) if t != normal_dir):
                    derivative[normal_dir, p, s] = slopes[point_idx[normal_dir], other_idx[normal_dir]]
    return (jnp.asarray(extrapolate, dtype=jnp.float32), jnp.asarray(derivative, dtype=jnp.float32),
            jnp.asarray(lifting, dtype=jnp.float32))


def face_values(solution, extrapolate):
    values = jnp.einsum('kp,vpe->vke', extrapolate, solution, precision=lax.Precision.HIGHEST)
    return values.reshape(values.shape[0], 16, 6 * values.shape[2])


def rim_buffer(surface_vals, speeds, links, faces_total, rim_count):
    slots = jnp.where(links >= faces_total, links - faces_total, 2 * rim_count)
    senders = jnp.zeros((2 * rim_count,), jnp.int32).at[slots].set(
        jnp.arange(faces_total, dtype=jnp.int32), mode="drop")
    return jnp.concatenate([jnp.take(surface_vals, senders, axis=2),
                            jnp.take(speeds, senders, axis=1)[None]], axis=0)


def surface_term(surface_vals, speeds, links, received, lifting, elems):
    table_vals = jnp.concatenate([surface_vals, received[:-1]], axis=2)
    table_speed = jnp.concatenate([speeds, received[-1]], axis=1)
    outer_vals = jnp.take(table_vals, links, axis=2)
    outer_speed = jnp.take(table_speed, links, axis=1)
    normal = 0.5 * (speeds - outer_speed)
    common = 0.5 * normal * (surface_vals + outer_vals) + 0.5 * jnp.abs(normal) * (surface_vals - outer_vals)
    jump_term = (common - speeds * surface_vals).reshape(surface_vals.shape[0], 96, elems)
    return jnp.einsum('pk,vke->vpe', lifting, jump_term, precision=lax.Precision.HIGHEST)


def volume_term(solution, velocity, derivative):
    slopes = jnp.einsum('dpq,vqe->dvpe', derivative, solution, precision=lax.Precision.HIGHEST)
    return jnp.sum(velocity[:, None, None, :] * slopes, axis=0)


def receptor_values(advanced, donors, coords):
    basis_x = jnp.stack(lagrange_at(coords[0]))
    basis_y = jnp.stack(lagrange_at(coords[1]))
    basis_z = jnp.stack(lagrange_at(coords[2]))
    weights = (basis_x[:, None, None, :] * basis_y[None, :, None, :] * basis_z[None, None, :, :]).reshape(64, -1)
    picked = jnp.take(advanced, donors, axis=2)
    return jnp.einsum('vpr,pr->vr', picked, weights, precision=lax.Precision.HIGHEST)


def owner_ranks(owners, buckets):
    onehot = (owners[:, None] == jnp.arange(buckets, dtype=jnp.int32)[None, :]).astype(jnp.int32)
    before = jnp.cumsum(onehot, axis=0) - onehot
    return jnp.sum(before * onehot, axis=1)


def reference(solution, velocity, inv_jacobian, face_speed, face_link, donor_elem, ref_coords, owner_list):
    extrapolate, derivative, lifting = tables()
    faces_total = 6 * E_DEV

    def device_slice(array, device):
        return lax.dynamic_slice_in_dim(array, device * E_DEV, E_DEV, array.ndim - 1)

    def outgoing_of(device):
        surface_vals = face_values(device_slice(solution, device), extrapolate)
        speeds = device_slice(face_speed, device).reshape(16, faces_total)
        links = device_slice(face_link, device).reshape(faces_total)
        return rim_buffer(surface_vals, speeds, links, faces_total, IFACE)

    devices_all = jnp.arange(DEVICES, dtype=jnp.int32)
    outgoing = lax.map(outgoing_of, devices_all)
    by_valve = outgoing.reshape(N_VALVE, N_BULK, 6, 16, 2 * IFACE)
    from_prev = jnp.roll(by_valve[..., IFACE:], 1, axis=0)
    from_next = jnp.roll(by_valve[..., :IFACE], -1, axis=0)
    incoming = jnp.concatenate([from_prev, from_next], axis=-1).reshape(DEVICES, 6, 16, 2 * IFACE)

    def section_of(packed):
        device, received = packed
        local_sol = device_slice(solution, device)
        surface_vals = face_values(local_sol, extrapolate)
        speeds = device_slice(face_speed, device).reshape(16, faces_total)
        links = device_slice(face_link, device).reshape(faces_total)
        surface = surface_term(surface_vals, speeds, links, received, lifting, E_DEV)
        volume = volume_term(local_sol, device_slice(velocity, device), derivative)
        rate = -device_slice(inv_jacobian, device)[None] * (volume + surface)
        advanced = local_sol + section_step * rate
        donors = lax.dynamic_slice_in_dim(donor_elem, device * REC_DEV, REC_DEV, 0)
        coords = lax.dynamic_slice_in_dim(ref_coords, device * REC_DEV, REC_DEV, 1)
        return rate, receptor_values(advanced, donors, coords)

    rates, receptor_vals = lax.map(section_of, (devices_all, incoming))
    section_rate = jnp.transpose(rates, (1, 2, 0, 3)).reshape(NVAR, SOLPTS, NEL)
    owners = owner_list[:, 0].reshape(N_VALVE * N_BULK, REC_DEV)
    ranks = jax.vmap(lambda row: owner_ranks(row, N_BULK))(owners).reshape(N_VALVE, N_BULK, REC_DEV)
    owners = owners.reshape(N_VALVE, N_BULK, REC_DEV)
    values = jnp.transpose(receptor_vals.reshape(N_VALVE, N_BULK, NVAR, REC_DEV), (2, 0, 1, 3))
    valve_idx = jnp.broadcast_to(jnp.arange(N_VALVE, dtype=jnp.int32)[:, None, None], owners.shape)
    places = jnp.arange(N_BULK, dtype=jnp.int32)[None, :, None] * CAP + ranks
    fringe = jnp.zeros((NVAR, N_VALVE, N_BULK, N_BULK * CAP), jnp.float32)
    fringe = fringe.at[:, valve_idx, owners, places].set(values)
    return section_rate, fringe.reshape(NVAR, SLOTS)
```

```python
import functools

import jax
import jax.numpy as jnp
import numpy as np
from jax import lax
from jax.experimental import pallas as pl
from jax.experimental.pallas import tpu as pltpu
from jax.sharding import PartitionSpec as P

gauss_nodes = (-0.8611363115940526, -0.3399810435848563, 0.3399810435848563, 0.8611363115940526)
quad_weights = (0.3478548451374538, 0.6521451548625461, 0.6521451548625461, 0.3478548451374538)
section_step = 0.2
MESH = pl.DeviceIdType.MESH
VMEM_BYTES = 48 * 1024 * 1024


def lagrange_at(x):
    values = []
    for j in range(4):
        factor = 1.0
        for m in range(4):
            if m != j:
                factor = factor * (x - gauss_nodes[m]) * (1.0 / (gauss_nodes[j] - gauss_nodes[m]))
        values.append(factor)
    return values


def tables():
    slopes = np.zeros((4, 4))
    for i in range(4):
        for j in range(4):
            summed = 0.0
            for m in range(4):
                if m != j:
                    product = 1.0 / (gauss_nodes[j] - gauss_nodes[m])
                    for n in range(4):
                        if n != j and n != m:
                            product = (
                                product
                                * (gauss_nodes[i] - gauss_nodes[n])
                                / (gauss_nodes[j] - gauss_nodes[n])
                            )
                    summed = summed + product
            slopes[i, j] = summed
    end_values = [lagrange_at(-1.0), lagrange_at(1.0)]
    extrapolate = np.zeros((96, 64))
    lifting = np.zeros((64, 96))
    derivative = np.zeros((3, 64, 64))
    for p in range(64):
        point_idx = (p // 16, p // 4 % 4, p % 4)
        for f in range(6):
            normal_dir = f // 2
            across = [t for t in range(3) if t != normal_dir]
            q = point_idx[across[0]] * 4 + point_idx[across[1]]
            flux_row = f * 16 + q
            extrapolate[flux_row, p] = end_values[f % 2][point_idx[normal_dir]]
            lifting[p, flux_row] = (
                end_values[f % 2][point_idx[normal_dir]] / quad_weights[point_idx[normal_dir]]
            )
        for s in range(64):
            other_idx = (s // 16, s // 4 % 4, s % 4)
            for normal_dir in range(3):
                if all((point_idx[t] == other_idx[t] for t in range(3) if t != normal_dir)):
                    derivative[normal_dir, p, s] = slopes[
                        point_idx[normal_dir], other_idx[normal_dir]
                    ]
    return extrapolate, derivative, lifting


def split_columns(matrix):
    matrix = np.asarray(matrix, np.float32)
    hi = matrix.astype(jnp.bfloat16)
    lo = (matrix - hi.astype(np.float32)).astype(jnp.bfloat16)
    return jnp.asarray(np.concatenate([hi, hi, lo], axis=1))


def halves(x):
    hi = x.astype(jnp.bfloat16)
    lo = (x - hi.astype(jnp.float32)).astype(jnp.bfloat16)
    return hi, lo


def split_rows(x):
    hi, lo = halves(x)
    return jnp.concatenate([hi, lo, hi], axis=0)


def dot(a, b):
    return jnp.dot(a, b, preferred_element_type=jnp.float32)


def dot_nt(a, b):
    return lax.dot_general(a, b, (((1,), (1,)), ((), ())), preferred_element_type=jnp.float32)


def by_face(speed_ref, tiles):
    count = tiles.shape[0]
    for t in range(count):
        tiles[t] = speed_ref[:, 128 * t : 128 * t + 128]
    return [
        jnp.concatenate([tiles[t, pl.ds(f, 16, stride=6), :] for t in range(count)], axis=1)
        for f in range(6)
    ]


def table_kernel(
    sol_ref, speed_ref, links_ref, ext_ref, table_ref, nat, tiles, out_rows, in_rows, send_sem, recv_sem
):
    nvars, _, elems = sol_ref.shape
    faces_total = 6 * elems
    rim = in_rows.shape[0] // 2
    size = lax.axis_size("valve")
    me = lax.axis_index("valve")
    up, down = lax.rem(me + 1, size), lax.rem(me + size - 1, size)
    barrier = pltpu.get_barrier_semaphore()
    for peer in (up, down):
        pl.semaphore_signal(barrier, inc=1, device_id={"valve": peer}, device_id_type=MESH)
    ext = ext_ref[...]
    speeds = by_face(speed_ref, tiles)
    for v in range(nvars):
        vals = dot(ext, split_rows(sol_ref[v]))
        for f in range(6):
            nat[f, 16 * v : 16 * v + 16, :] = vals[16 * f : 16 * f + 16]
    picked = jnp.zeros((2 * rim, 128), jnp.float32)
    slot = lax.broadcasted_iota(jnp.int32, (2 * rim, elems), 0) + faces_total
    for f in range(6):
        nat[f, 16 * nvars : 16 * nvars + 16, :] = speeds[f]
        nat[f, 16 * nvars + 16 :, :] = jnp.zeros((112 - 16 * nvars, elems), jnp.float32)
        rows = nat[f].T
        table_ref[f * elems : (f + 1) * elems, :] = rows
        onehot = (links_ref[f : f + 1, :] == slot).astype(jnp.float32).astype(jnp.bfloat16)
        hi, lo = halves(rows)
        picked = picked + dot(onehot, hi) + dot(onehot, lo)
    out_rows[...] = picked
    pl.semaphore_wait(barrier, 2)
    to_up = pltpu.make_async_remote_copy(
        src_ref=out_rows.at[rim:],
        dst_ref=in_rows.at[:rim],
        send_sem=send_sem.at[0],
        recv_sem=recv_sem.at[0],
        device_id={"valve": up},
        device_id_type=MESH,
    )
    to_down = pltpu.make_async_remote_copy(
        src_ref=out_rows.at[:rim],
        dst_ref=in_rows.at[rim:],
        send_sem=send_sem.at[1],
        recv_sem=recv_sem.at[1],
        device_id={"valve": down},
        device_id_type=MESH,
    )
    to_up.start()
    to_down.start()
    to_up.wait()
    to_down.wait()
    table_ref[faces_total:, :] = in_rows[...]


def face_table(solution, face_speed, face_link, extrapolate):
    elems = solution.shape[2]
    rim = elems // 16
    vmem = pl.BlockSpec(memory_space=pltpu.VMEM)
    return pl.pallas_call(
        table_kernel,
        out_shape=jax.ShapeDtypeStruct((6 * elems + 2 * rim, 128), jnp.float32),
        in_specs=[vmem] * 4,
        out_specs=vmem,
        scratch_shapes=[
            pltpu.VMEM((6, 128, elems), jnp.float32),
            pltpu.VMEM((elems // 128, 96, 128), jnp.float32),
            pltpu.VMEM((2 * rim, 128), jnp.float32),
            pltpu.VMEM((2 * rim, 128), jnp.float32),
            pltpu.SemaphoreType.DMA((2,)),
            pltpu.SemaphoreType.DMA((2,)),
        ],
        compiler_params=pltpu.CompilerParams(
            collective_id=0, has_side_effects=True, vmem_limit_bytes=VMEM_BYTES
        ),
        name="face_table",
    )(solution, face_speed, face_link, extrapolate)


def section_kernel(
    links_ref, table_ref, sol_ref, vel_ref, jac_ref, speed_ref, ops_ref, lift_ref,
    rate_ref, hi_ref, lo_ref, rows, jump, tiles,
):
    nvars, _, width = sol_ref.shape
    start = pl.program_id(0) * width
    step = 16

    def gather(i, carry):
        base = pl.multiple_of(i * step, step)
        for f in range(6):
            for u in range(step):
                link = links_ref[f, start + base + u]
                rows[f, pl.ds(base + u, 1), :] = table_ref[pl.ds(link, 1), :]
        return carry

    lax.fori_loop(0, width // step, gather, 0)
    ops = ops_ref[...]
    vel = vel_ref[...]
    speeds = by_face(speed_ref, tiles)
    own = [dot(ops, split_rows(sol_ref[v])) for v in range(nvars)]
    for f in range(6):
        outer = rows[f].T
        speed = speeds[f]
        normal = 0.5 * (speed - outer[16 * nvars : 16 * nvars + 16])
        mean, diff = 0.5 * normal, 0.5 * jnp.abs(normal)
        for v in range(nvars):
            inner = own[v][16 * f : 16 * f + 16]
            other = outer[16 * v : 16 * v + 16]
            jump[v, 16 * f : 16 * f + 16, :] = (
                mean * (inner + other) + diff * (inner - other) - speed * inner
            )
    lift = lift_ref[...]
    jac = jac_ref[...]
    for v in range(nvars):
        total = dot(lift, split_rows(jump[v]))
        for d in range(3):
            total = total + vel[d : d + 1] * own[v][96 + 64 * d : 160 + 64 * d]
        rate = -jac * total
        rate_ref[v] = rate
        hi, lo = halves(sol_ref[v] + section_step * rate)
        hi_ref[64 * v : 64 * v + 64, :] = hi
        lo_ref[64 * v : 64 * v + 64, :] = lo


def section(face_link, table, solution, velocity, inv_jacobian, face_speed, operators, lifting):
    nvars, points, elems = solution.shape
    width = 256
    whole = lambda shape: pl.BlockSpec(shape, lambda i, links: (0,) * len(shape))
    block = lambda rows: pl.BlockSpec((rows, width), lambda i, links: (0, i))
    cube = pl.BlockSpec((nvars, points, width), lambda i, links: (0, 0, i))
    pieces = jax.ShapeDtypeStruct((nvars * points, elems), jnp.bfloat16)
    return pl.pallas_call(
        section_kernel,
        grid_spec=pltpu.PrefetchScalarGridSpec(
            num_scalar_prefetch=1,
            grid=(elems // width,),
            in_specs=[
                whole(table.shape), cube, block(3), block(64), block(96),
                whole(operators.shape), whole(lifting.shape),
            ],
            out_specs=[cube, block(nvars * points), block(nvars * points)],
            scratch_shapes=[
                pltpu.VMEM((6, width, 128), jnp.float32),
                pltpu.VMEM((nvars, 96, width), jnp.float32),
                pltpu.VMEM((width // 128, 96, 128), jnp.float32),
            ],
        ),
        out_shape=[jax.ShapeDtypeStruct(solution.shape, jnp.float32), pieces, pieces],
        compiler_params=pltpu.CompilerParams(vmem_limit_bytes=VMEM_BYTES),
        name="section",
    )(face_link, table, solution, velocity, inv_jacobian, face_speed, operators, lifting)


def receptor_kernel(buckets, nvars, hi_ref, lo_ref, donor_ref, coord_ref, owner_ref, out_ref, pieces, acc, seen, upper):
    elems = hi_ref.shape[1]
    width = donor_ref.shape[1]
    capacity = 16384 // buckets
    step = pl.program_id(0)
    rows = nvars * 64

    @pl.when(step == 0)
    def _():
        pieces[:rows, :] = hi_ref[...]
        pieces[rows:, :] = lo_ref[...]
        seen[...] = jnp.zeros_like(seen)
        upper[...] = (
            lax.broadcasted_iota(jnp.int32, (width, width), 0)
            < lax.broadcasted_iota(jnp.int32, (width, width), 1)
        ).astype(jnp.float32).astype(jnp.bfloat16)

    donor = donor_ref[...]
    chosen = (lax.broadcasted_iota(jnp.int32, (elems, width), 0) == donor)
    chosen = chosen.astype(jnp.float32).astype(jnp.bfloat16)
    picked = dot(pieces[...], chosen)
    lx = lagrange_at(coord_ref[0:1, :])
    ly = lagrange_at(coord_ref[1:2, :])
    lz = jnp.concatenate(lagrange_at(coord_ref[2:3, :]), axis=0)
    yz = jnp.concatenate([ly[j] * lz for j in range(4)], axis=0)
    weights = jnp.concatenate([lx[i] * yz for i in range(4)], axis=0)
    values = []
    for v in range(nvars):
        both = picked[64 * v : 64 * v + 64] + picked[rows + 64 * v : rows + 64 * v + 64]
        values.append(jnp.sum(both * weights, axis=0, keepdims=True))

    owner = owner_ref[...]
    named = (lax.broadcasted_iota(jnp.int32, (16, width), 0) == owner).astype(jnp.float32)
    before = dot(named.astype(jnp.bfloat16), upper[...]) + seen[:, 0:1]
    rank = jnp.sum(named * before, axis=0, keepdims=True)
    seen[...] = seen[...] + jnp.sum(named, axis=1, keepdims=True)
    place = owner * capacity + rank.astype(jnp.int32)
    in_row = (lax.broadcasted_iota(jnp.int32, (64, width), 0) == place // 256)
    in_row = in_row.astype(jnp.float32).astype(jnp.bfloat16)
    in_lane = (lax.broadcasted_iota(jnp.int32, (256, width), 0) == lax.rem(place, 256))
    in_lane = in_lane.astype(jnp.float32).astype(jnp.bfloat16)
    parts = []
    for v in range(nvars):
        for piece in halves(values[v]):
            parts.append(in_row * piece)
    spread = dot_nt(jnp.concatenate(parts, axis=0), in_lane)
    acc[...] = jnp.where(step == 0, 0.0, acc[...]) + spread

    @pl.when(step == pl.num_programs(0) - 1)
    def _():
        for v in range(nvars):
            both = acc[128 * v : 128 * v + 64, :] + acc[128 * v + 64 : 128 * v + 128, :]
            out_ref[pl.ds(v, 64, stride=2 * nvars), :] = both[:, :128]
            out_ref[pl.ds(nvars + v, 64, stride=2 * nvars), :] = both[:, 128:]


def receptor_slots(hi, lo, donors, coords, owners, buckets):
    rows, elems = hi.shape
    nvars = rows // 64
    receptors = donors.shape[1]
    width = 512
    whole = pl.BlockSpec((rows, elems), lambda i: (0, 0))
    block = lambda count: pl.BlockSpec((count, width), lambda i: (0, i))
    return pl.pallas_call(
        functools.partial(receptor_kernel, buckets, nvars),
        grid=(receptors // width,),
        in_specs=[whole, whole, block(1), block(3), block(1)],
        out_specs=pl.BlockSpec((nvars * 128, 128), lambda i: (0, 0)),
        out_shape=jax.ShapeDtypeStruct((nvars * 128, 128), jnp.float32),
        scratch_shapes=[
            pltpu.VMEM((2 * rows, elems), jnp.bfloat16),
            pltpu.VMEM((128 * nvars, 256), jnp.float32),
            pltpu.VMEM((16, 128), jnp.float32),
            pltpu.VMEM((width, width), jnp.bfloat16),
        ],
        compiler_params=pltpu.CompilerParams(vmem_limit_bytes=VMEM_BYTES),
        name="receptor_slots",
    )(hi, lo, donors, coords, owners)


def exchange_kernel(buckets, nvars, send_ref, out_ref, held, send_sem, recv_sem):
    block = nvars * 128 // buckets
    me = lax.axis_index("bulk")
    barrier = pltpu.get_barrier_semaphore()
    peers = [lax.rem(me + k, buckets) for k in range(1, buckets)]
    for peer in peers:
        pl.semaphore_signal(barrier, inc=1, device_id={"bulk": peer}, device_id_type=MESH)
    pl.semaphore_wait(barrier, buckets - 1)
    mine = pl.ds(pl.multiple_of(me * block, 8), block)
    copies = []
    for k, peer in enumerate(peers):
        copy = pltpu.make_async_remote_copy(
            src_ref=send_ref.at[pl.ds(pl.multiple_of(peer * block, 8), block)],
            dst_ref=held.at[mine],
            send_sem=send_sem.at[k],
            recv_sem=recv_sem.at[k],
            device_id={"bulk": peer},
            device_id_type=MESH,
        )
        copy.start()
        copies.append(copy)
    held[mine, :] = send_ref[mine, :]
    for copy in copies:
        copy.wait()
    for j in range(128):
        out_ref[:, 128 * j : 128 * j + 128] = held[nvars * j : nvars * j + nvars, :]


def exchange(slots, nvars, buckets):
    vmem = pl.BlockSpec(memory_space=pltpu.VMEM)
    return pl.pallas_call(
        functools.partial(exchange_kernel, buckets, nvars),
        out_shape=jax.ShapeDtypeStruct((nvars, 16384), jnp.float32),
        in_specs=[vmem],
        out_specs=vmem,
        scratch_shapes=[
            pltpu.VMEM(slots.shape, jnp.float32),
            pltpu.SemaphoreType.DMA((buckets - 1,)),
            pltpu.SemaphoreType.DMA((buckets - 1,)),
        ],
        compiler_params=pltpu.CompilerParams(
            collective_id=1, has_side_effects=True, vmem_limit_bytes=VMEM_BYTES
        ),
        name="exchange",
    )(slots)


def on_device(
    solution, velocity, inv_jacobian, face_speed, face_link, donor_elem, ref_coords, owner_list
):
    extrapolate, derivative, lifting = tables()
    nvars = solution.shape[0]
    buckets = lax.axis_size("bulk")
    operators = np.concatenate([extrapolate, derivative.reshape(192, 64)], axis=0)
    table = face_table(solution, face_speed, face_link, split_columns(extrapolate))
    section_rate, hi, lo = section(
        face_link, table, solution, velocity, inv_jacobian, face_speed,
        split_columns(operators), split_columns(lifting),
    )
    slots = receptor_slots(
        hi, lo, donor_elem.reshape(1, -1), ref_coords, owner_list.reshape(1, -1), buckets
    )
    return (section_rate, exchange(slots, nvars, buckets))


def solution(mesh):
    placed = (
        P(None, None, ("valve", "bulk")),
        P(None, ("valve", "bulk")),
        P(None, ("valve", "bulk")),
        P(None, ("valve", "bulk")),
        P(None, ("valve", "bulk")),
        P(("valve", "bulk")),
        P(None, ("valve", "bulk")),
        P(("valve", "bulk"), None),
    )
    return jax.shard_map(
        on_device,
        mesh=mesh,
        in_specs=placed,
        out_specs=(P(None, None, ("valve", "bulk")), P(None, ("valve", "bulk"))),
        check_vma=False,
    )
```

```python
import functools

import jax
import jax.numpy as jnp
import numpy as np
from jax import lax
from jax.experimental import pallas as pl
from jax.experimental.pallas import tpu as pltpu
from jax.sharding import PartitionSpec as P

gauss_nodes = (-0.8611363115940526, -0.3399810435848563, 0.3399810435848563, 0.8611363115940526)
quad_weights = (0.3478548451374538, 0.6521451548625461, 0.6521451548625461, 0.3478548451374538)
section_step = 0.2
MESH = pl.DeviceIdType.MESH
VMEM_BYTES = 56 * 1024 * 1024


def lagrange_at(x):
    values = []
    for j in range(4):
        factor = 1.0
        for m in range(4):
            if m != j:
                factor = factor * (x - gauss_nodes[m]) * (1.0 / (gauss_nodes[j] - gauss_nodes[m]))
        values.append(factor)
    return values


def tables():
    slopes = np.zeros((4, 4))
    for i in range(4):
        for j in range(4):
            summed = 0.0
            for m in range(4):
                if m != j:
                    product = 1.0 / (gauss_nodes[j] - gauss_nodes[m])
                    for n in range(4):
                        if n != j and n != m:
                            product = (
                                product
                                * (gauss_nodes[i] - gauss_nodes[n])
                                / (gauss_nodes[j] - gauss_nodes[n])
                            )
                    summed = summed + product
            slopes[i, j] = summed
    end_values = [lagrange_at(-1.0), lagrange_at(1.0)]
    extrapolate = np.zeros((96, 64))
    lifting = np.zeros((64, 96))
    derivative = np.zeros((3, 64, 64))
    for p in range(64):
        point_idx = (p // 16, p // 4 % 4, p % 4)
        for f in range(6):
            normal_dir = f // 2
            across = [t for t in range(3) if t != normal_dir]
            q = point_idx[across[0]] * 4 + point_idx[across[1]]
            flux_row = f * 16 + q
            extrapolate[flux_row, p] = end_values[f % 2][point_idx[normal_dir]]
            lifting[p, flux_row] = (
                end_values[f % 2][point_idx[normal_dir]] / quad_weights[point_idx[normal_dir]]
            )
        for s in range(64):
            other_idx = (s // 16, s // 4 % 4, s % 4)
            for normal_dir in range(3):
                if all((point_idx[t] == other_idx[t] for t in range(3) if t != normal_dir)):
                    derivative[normal_dir, p, s] = slopes[
                        point_idx[normal_dir], other_idx[normal_dir]
                    ]
    return extrapolate, derivative, lifting


def split_columns(matrix):
    matrix = np.asarray(matrix, np.float32)
    hi = matrix.astype(jnp.bfloat16)
    lo = (matrix - hi.astype(np.float32)).astype(jnp.bfloat16)
    return jnp.asarray(np.concatenate([hi, hi, lo], axis=1))


def halves(x):
    hi = x.astype(jnp.bfloat16)
    lo = (x - hi.astype(jnp.float32)).astype(jnp.bfloat16)
    return hi, lo


def split_rows(x):
    hi, lo = halves(x)
    return jnp.concatenate([hi, lo, hi], axis=0)


def dot(a, b):
    return jnp.dot(a, b, preferred_element_type=jnp.float32)


def dot_nt(a, b):
    return lax.dot_general(a, b, (((1,), (1,)), ((), ())), preferred_element_type=jnp.float32)


def by_face(speed_ref, tiles):
    count = tiles.shape[0]
    for t in range(count):
        tiles[t] = speed_ref[:, 128 * t : 128 * t + 128]
    return [
        jnp.concatenate([tiles[t, pl.ds(f, 16, stride=6), :] for t in range(count)], axis=1)
        for f in range(6)
    ]


def table_kernel(
    sol_hbm, speed_hbm, links_hbm, ext_ref, table_ref,
    sol_ref, speed_ref, links_ref, nat, tiles, out_rows, in_rows, fetch_sem, send_sem, recv_sem,
):
    nvars, _, elems = sol_ref.shape
    fetches = [pltpu.make_async_copy(speed_hbm, speed_ref, fetch_sem.at[nvars])]
    for v in range(nvars):
        fetches.append(pltpu.make_async_copy(sol_hbm.at[v], sol_ref.at[v], fetch_sem.at[v]))
    fetches.append(pltpu.make_async_copy(links_hbm, links_ref, fetch_sem.at[nvars + 1]))
    for fetch in fetches:
        fetch.start()
    faces_total = 6 * elems
    rim = in_rows.shape[0] // 2
    size = lax.axis_size("valve")
    me = lax.axis_index("valve")
    up, down = lax.rem(me + 1, size), lax.rem(me + size - 1, size)
    barrier = pltpu.get_barrier_semaphore()
    for peer in (up, down):
        pl.semaphore_signal(barrier, inc=1, device_id={"valve": peer}, device_id_type=MESH)
    ext = ext_ref[...]
    fetches[0].wait()
    speeds = by_face(speed_ref, tiles)
    for v in range(nvars):
        fetches[v + 1].wait()
        vals = dot(ext, split_rows(sol_ref[v]))
        for f in range(6):
            nat[f, 16 * v : 16 * v + 16, :] = vals[16 * f : 16 * f + 16]
    fetches[nvars + 1].wait()
    picked = jnp.zeros((2 * rim, 128), jnp.float32)
    slot = lax.broadcasted_iota(jnp.int32, (2 * rim, elems), 0) + faces_total
    for f in range(6):
        nat[f, 16 * nvars : 16 * nvars + 16, :] = speeds[f]
        nat[f, 16 * nvars + 16 :, :] = jnp.zeros((112 - 16 * nvars, elems), jnp.float32)
        rows = nat[f].T
        table_ref[f * elems : (f + 1) * elems, :] = rows
        onehot = (links_ref[f : f + 1, :] == slot).astype(jnp.float32).astype(jnp.bfloat16)
        hi, lo = halves(rows)
        picked = picked + dot(onehot, hi) + dot(onehot, lo)
    out_rows[...] = picked
    pl.semaphore_wait(barrier, 2)
    to_up = pltpu.make_async_remote_copy(
        src_ref=out_rows.at[rim:],
        dst_ref=in_rows.at[:rim],
        send_sem=send_sem.at[0],
        recv_sem=recv_sem.at[0],
        device_id={"valve": up},
        device_id_type=MESH,
    )
    to_down = pltpu.make_async_remote_copy(
        src_ref=out_rows.at[:rim],
        dst_ref=in_rows.at[rim:],
        send_sem=send_sem.at[1],
        recv_sem=recv_sem.at[1],
        device_id={"valve": down},
        device_id_type=MESH,
    )
    to_up.start()
    to_down.start()
    to_up.wait()
    to_down.wait()
    table_ref[faces_total:, :] = in_rows[...]


def face_table(solution, face_speed, face_link, extrapolate):
    elems = solution.shape[2]
    rim = elems // 16
    vmem = pl.BlockSpec(memory_space=pltpu.VMEM)
    return pl.pallas_call(
        table_kernel,
        out_shape=jax.ShapeDtypeStruct((6 * elems + 2 * rim, 128), jnp.float32),
        in_specs=[pl.BlockSpec(memory_space=pl.ANY)] * 3 + [vmem],
        out_specs=vmem,
        scratch_shapes=[
            pltpu.VMEM(solution.shape, jnp.float32),
            pltpu.VMEM(face_speed.shape, jnp.float32),
            pltpu.VMEM(face_link.shape, jnp.int32),
            pltpu.VMEM((6, 128, elems), jnp.float32),
            pltpu.VMEM((elems // 128, 96, 128), jnp.float32),
            pltpu.VMEM((2 * rim, 128), jnp.float32),
            pltpu.VMEM((2 * rim, 128), jnp.float32),
            pltpu.SemaphoreType.DMA((solution.shape[0] + 2,)),
            pltpu.SemaphoreType.DMA((2,)),
            pltpu.SemaphoreType.DMA((2,)),
        ],
        compiler_params=pltpu.CompilerParams(
            collective_id=0, has_side_effects=True, vmem_limit_bytes=VMEM_BYTES
        ),
        name="face_table",
    )(solution, face_speed, face_link, extrapolate)


def section_kernel(
    links_ref, table_ref, sol_ref, vel_ref, jac_ref, speed_ref, ops_ref, lift_ref,
    rate_ref, hi_ref, lo_ref, even, odd, jump, tiles,
):
    nvars, _, width = sol_ref.shape
    half = 128
    step = pl.program_id(0)
    last = pl.num_programs(0) * width - half
    ops = ops_ref[...]
    lift = lift_ref[...]

    def fetch(rows, f, u, start):
        rows[f, pl.ds(u, 1), :] = table_ref[pl.ds(links_ref[f, start + u], 1), :]

    @pl.when(step == 0)
    def _():
        def eight(i, carry):
            for f in range(6):
                for u in range(8):
                    fetch(even, f, pl.multiple_of(8 * i, 8) + u, 0)
            return carry

        lax.fori_loop(0, half // 8, eight, 0)

    def work(rows, span, coming, start):
        vel = vel_ref[:, span]
        jac = jac_ref[:, span]
        tiles[...] = speed_ref[:, span]
        sol = [sol_ref[v, :, span] for v in range(nvars)]
        own = [dot(ops, split_rows(sol[v])) for v in range(nvars)]
        for f in range(6):
            for u in range(half):
                fetch(coming, f, u, start)
            outer = rows[f].T
            speed = tiles[pl.ds(f, 16, stride=6), :]
            normal = 0.5 * (speed - outer[16 * nvars : 16 * nvars + 16])
            mean, diff = 0.5 * normal, 0.5 * jnp.abs(normal)
            for v in range(nvars):
                inner = own[v][16 * f : 16 * f + 16]
                other = outer[16 * v : 16 * v + 16]
                jump[v, 16 * f : 16 * f + 16, :] = (
                    mean * (inner + other) + diff * (inner - other) - speed * inner
                )
        for v in range(nvars):
            total = dot(lift, split_rows(jump[v]))
            for d in range(3):
                total = total + vel[d : d + 1] * own[v][96 + 64 * d : 160 + 64 * d]
            rate = -jac * total
            rate_ref[v, :, span] = rate
            hi, lo = halves(sol[v] + section_step * rate)
            hi_ref[64 * v : 64 * v + 64, span] = hi
            lo_ref[64 * v : 64 * v + 64, span] = lo

    base = step * width
    work(even, slice(0, half), odd, base + half)
    work(odd, slice(half, 2 * half), even, jnp.minimum(base + 2 * half, last))


def section(face_link, table, solution, velocity, inv_jacobian, face_speed, operators, lifting):
    nvars, points, elems = solution.shape
    width = 256
    whole = pl.BlockSpec(memory_space=pltpu.VMEM)
    block = lambda rows: pl.BlockSpec((rows, width), lambda i, links: (0, i))
    cube = pl.BlockSpec((nvars, points, width), lambda i, links: (0, 0, i))
    pieces = jax.ShapeDtypeStruct((nvars * points, elems), jnp.bfloat16)
    return pl.pallas_call(
        section_kernel,
        grid_spec=pltpu.PrefetchScalarGridSpec(
            num_scalar_prefetch=1,
            grid=(elems // width,),
            in_specs=[whole, cube, block(3), block(64), block(96), whole, whole],
            out_specs=[cube, block(nvars * points), block(nvars * points)],
            scratch_shapes=[
                pltpu.VMEM((6, 128, 128), jnp.float32),
                pltpu.VMEM((6, 128, 128), jnp.float32),
                pltpu.VMEM((nvars, 96, 128), jnp.float32),
                pltpu.VMEM((96, 128), jnp.float32),
            ],
        ),
        out_shape=[jax.ShapeDtypeStruct(solution.shape, jnp.float32), pieces, pieces],
        compiler_params=pltpu.CompilerParams(vmem_limit_bytes=VMEM_BYTES),
        name="section",
    )(face_link, table, solution, velocity, inv_jacobian, face_speed, operators, lifting)


def one_hot(rows, index, dtype=jnp.int16):
    count = lax.broadcasted_iota(dtype, (rows, index.shape[1]), 0)
    return jnp.where(count == index.astype(dtype), jnp.bfloat16(1), jnp.bfloat16(0))


def receptor_kernel(buckets, nvars, hi_ref, lo_ref, donor_ref, coord_ref, owner_ref, out_ref, pieces, acc, seen):
    elems = hi_ref.shape[1]
    width = donor_ref.shape[1]
    part = 512
    tile = 256
    capacity = 16384 // buckets
    step = pl.program_id(0)
    rows = nvars * 64

    @pl.when(step == 0)
    def _():
        pieces[:rows, :] = hi_ref[...]
        pieces[rows:, :] = lo_ref[...]

    owner = owner_ref[...]
    named = (lax.broadcasted_iota(jnp.int32, (16, width), 0) == owner).astype(jnp.float32)
    upper = (
        lax.broadcasted_iota(jnp.int32, (tile, tile), 0)
        < lax.broadcasted_iota(jnp.int32, (tile, tile), 1)
    ).astype(jnp.float32).astype(jnp.bfloat16)
    tiles = [named[:, t : t + tile] for t in range(0, width, tile)]
    before = dot(jnp.concatenate(tiles, axis=0).astype(jnp.bfloat16), upper)
    carry = jnp.where(step == 0, 0.0, seen[...])[:, 0:1]
    ranks = []
    for t, own in enumerate(tiles):
        ranks.append(jnp.sum(own * (before[16 * t : 16 * t + 16] + carry), axis=0, keepdims=True))
        carry = carry + jnp.sum(own, axis=1, keepdims=True)
    seen[...] = jnp.broadcast_to(carry, seen.shape)
    place = owner * capacity + jnp.concatenate(ranks, axis=1).astype(jnp.int32)
    in_row = one_hot(64, place // 256)
    in_lane = one_hot(256, lax.rem(place, 256))

    both_pieces = pieces[...]
    columns = []
    for start in range(0, width, part):
        span = slice(start, start + part)
        picked = dot(both_pieces, one_hot(elems, donor_ref[:, span]))
        lx = lagrange_at(coord_ref[0:1, span])
        ly = lagrange_at(coord_ref[1:2, span])
        lz = jnp.concatenate(lagrange_at(coord_ref[2:3, span]), axis=0)
        yz = jnp.concatenate([ly[j] * lz for j in range(4)], axis=0)
        weights = jnp.concatenate([lx[i] * yz for i in range(4)], axis=0)
        parts = []
        for v in range(nvars):
            both = picked[64 * v : 64 * v + 64] + picked[rows + 64 * v : rows + 64 * v + 64]
            value = jnp.sum(both * weights, axis=0, keepdims=True)
            for piece in halves(value):
                parts.append(in_row[:, span] * piece)
        columns.append(jnp.concatenate(parts, axis=0))
    spread = dot_nt(jnp.concatenate(columns, axis=1), in_lane)
    acc[...] = jnp.where(step == 0, 0.0, acc[...]) + spread

    @pl.when(step == pl.num_programs(0) - 1)
    def _():
        for v in range(nvars):
            both = acc[128 * v : 128 * v + 64, :] + acc[128 * v + 64 : 128 * v + 128, :]
            out_ref[pl.ds(v, 64, stride=2 * nvars), :] = both[:, :128]
            out_ref[pl.ds(nvars + v, 64, stride=2 * nvars), :] = both[:, 128:]


def receptor_slots(hi, lo, donors, coords, owners, buckets):
    rows, elems = hi.shape
    nvars = rows // 64
    receptors = donors.shape[1]
    width = 2048
    whole = pl.BlockSpec(memory_space=pltpu.VMEM)
    block = lambda count: pl.BlockSpec((count, width), lambda i: (0, i))
    return pl.pallas_call(
        functools.partial(receptor_kernel, buckets, nvars),
        grid=(receptors // width,),
        in_specs=[whole, whole, block(1), block(3), block(1)],
        out_specs=pl.BlockSpec((nvars * 128, 128), lambda i: (0, 0)),
        out_shape=jax.ShapeDtypeStruct((nvars * 128, 128), jnp.float32),
        scratch_shapes=[
            pltpu.VMEM((2 * rows, elems), jnp.bfloat16),
            pltpu.VMEM((128 * nvars, 256), jnp.float32),
            pltpu.VMEM((16, 128), jnp.float32),
        ],
        compiler_params=pltpu.CompilerParams(vmem_limit_bytes=VMEM_BYTES),
        name="receptor_slots",
    )(hi, lo, donors, coords, owners)


def exchange_kernel(buckets, nvars, send_ref, out_ref, held, send_sem, recv_sem):
    block = nvars * 128 // buckets
    me = lax.axis_index("bulk")
    barrier = pltpu.get_barrier_semaphore()
    peers = [lax.rem(me + k, buckets) for k in range(1, buckets)]
    for peer in peers:
        pl.semaphore_signal(barrier, inc=1, device_id={"bulk": peer}, device_id_type=MESH)
    pl.semaphore_wait(barrier, buckets - 1)
    mine = pl.ds(pl.multiple_of(me * block, 8), block)
    copies = []
    for k, peer in enumerate(peers):
        copy = pltpu.make_async_remote_copy(
            src_ref=send_ref.at[pl.ds(pl.multiple_of(peer * block, 8), block)],
            dst_ref=held.at[mine],
            send_sem=send_sem.at[k],
            recv_sem=recv_sem.at[k],
            device_id={"bulk": peer},
            device_id_type=MESH,
        )
        copy.start()
        copies.append(copy)
    held[mine, :] = send_ref[mine, :]
    for copy in copies:
        copy.wait()
    for j in range(128):
        out_ref[:, 128 * j : 128 * j + 128] = held[nvars * j : nvars * j + nvars, :]


def exchange(slots, nvars, buckets):
    vmem = pl.BlockSpec(memory_space=pltpu.VMEM)
    return pl.pallas_call(
        functools.partial(exchange_kernel, buckets, nvars),
        out_shape=jax.ShapeDtypeStruct((nvars, 16384), jnp.float32),
        in_specs=[vmem],
        out_specs=vmem,
        scratch_shapes=[
            pltpu.VMEM(slots.shape, jnp.float32),
            pltpu.SemaphoreType.DMA((buckets - 1,)),
            pltpu.SemaphoreType.DMA((buckets - 1,)),
        ],
        compiler_params=pltpu.CompilerParams(
            collective_id=1, has_side_effects=True, vmem_limit_bytes=VMEM_BYTES
        ),
        name="exchange",
    )(slots)


def on_device(
    solution, velocity, inv_jacobian, face_speed, face_link, donor_elem, ref_coords, owner_list
):
    extrapolate, derivative, lifting = tables()
    nvars = solution.shape[0]
    buckets = lax.axis_size("bulk")
    operators = np.concatenate([extrapolate, derivative.reshape(192, 64)], axis=0)
    table = face_table(solution, face_speed, face_link, split_columns(extrapolate))
    section_rate, hi, lo = section(
        face_link, table, solution, velocity, inv_jacobian, face_speed,
        split_columns(operators), split_columns(lifting),
    )
    slots = receptor_slots(
        hi, lo, donor_elem.reshape(1, -1), ref_coords, owner_list.reshape(1, -1), buckets
    )
    return (section_rate, exchange(slots, nvars, buckets))


def solution(mesh):
    placed = (
        P(None, None, ("valve", "bulk")),
        P(None, ("valve", "bulk")),
        P(None, ("valve", "bulk")),
        P(None, ("valve", "bulk")),
        P(None, ("valve", "bulk")),
        P(("valve", "bulk")),
        P(None, ("valve", "bulk")),
        P(("valve", "bulk"), None),
    )
    return jax.shard_map(
        on_device,
        mesh=mesh,
        in_specs=placed,
        out_specs=(P(None, None, ("valve", "bulk")), P(None, ("valve", "bulk"))),
        check_vma=False,
    )
```

```python
import functools

import jax
import jax.numpy as jnp
import numpy as np
from jax import lax
from jax.experimental import pallas as pl
from jax.experimental.pallas import tpu as pltpu
from jax.sharding import PartitionSpec as P

gauss_nodes = (-0.8611363115940526, -0.3399810435848563, 0.3399810435848563, 0.8611363115940526)
quad_weights = (0.3478548451374538, 0.6521451548625461, 0.6521451548625461, 0.3478548451374538)
section_step = 0.2
MESH = pl.DeviceIdType.MESH
VMEM_BYTES = 32 * 1024 * 1024


def lagrange_at(x):
    values = []
    for j in range(4):
        factor = 1.0
        for m in range(4):
            if m != j:
                factor = factor * (x - gauss_nodes[m]) * (1.0 / (gauss_nodes[j] - gauss_nodes[m]))
        values.append(factor)
    return values


def tables():
    slopes = np.zeros((4, 4))
    for i in range(4):
        for j in range(4):
            summed = 0.0
            for m in range(4):
                if m != j:
                    product = 1.0 / (gauss_nodes[j] - gauss_nodes[m])
                    for n in range(4):
                        if n != j and n != m:
                            product = (
                                product
                                * (gauss_nodes[i] - gauss_nodes[n])
                                / (gauss_nodes[j] - gauss_nodes[n])
                            )
                    summed = summed + product
            slopes[i, j] = summed
    end_values = [lagrange_at(-1.0), lagrange_at(1.0)]
    extrapolate = np.zeros((96, 64))
    lifting = np.zeros((64, 96))
    derivative = np.zeros((3, 64, 64))
    for p in range(64):
        point_idx = (p // 16, p // 4 % 4, p % 4)
        for f in range(6):
            normal_dir = f // 2
            across = [t for t in range(3) if t != normal_dir]
            q = point_idx[across[0]] * 4 + point_idx[across[1]]
            flux_row = f * 16 + q
            extrapolate[flux_row, p] = end_values[f % 2][point_idx[normal_dir]]
            lifting[p, flux_row] = (
                end_values[f % 2][point_idx[normal_dir]] / quad_weights[point_idx[normal_dir]]
            )
        for s in range(64):
            other_idx = (s // 16, s // 4 % 4, s % 4)
            for normal_dir in range(3):
                if all((point_idx[t] == other_idx[t] for t in range(3) if t != normal_dir)):
                    derivative[normal_dir, p, s] = slopes[
                        point_idx[normal_dir], other_idx[normal_dir]
                    ]
    return extrapolate, derivative, lifting


def split_columns(matrix):
    matrix = np.asarray(matrix, np.float32)
    hi = matrix.astype(jnp.bfloat16)
    lo = (matrix - hi.astype(np.float32)).astype(jnp.bfloat16)
    return jnp.asarray(np.concatenate([hi, hi, lo], axis=1))


def halves(x):
    hi = x.astype(jnp.bfloat16)
    lo = (x - hi.astype(jnp.float32)).astype(jnp.bfloat16)
    return hi, lo


def split_rows(x):
    hi, lo = halves(x)
    return jnp.concatenate([hi, lo, hi], axis=0)


def dot(a, b):
    return jnp.dot(a, b, preferred_element_type=jnp.float32)


def dot_nt(a, b):
    return lax.dot_general(a, b, (((1,), (1,)), ((), ())), preferred_element_type=jnp.float32)


def by_face(speed_ref, tiles):
    count = tiles.shape[0]
    for t in range(count):
        tiles[t] = speed_ref[:, 128 * t : 128 * t + 128]
    return [
        jnp.concatenate([tiles[t, pl.ds(f, 16, stride=6), :] for t in range(count)], axis=1)
        for f in range(6)
    ]


def table_kernel(
    sol_ref, speed_ref, links_ref, ext_ref, table_ref, nat, tiles, out_rows, in_rows, send_sem, recv_sem
):
    nvars, _, elems = sol_ref.shape
    faces_total = 6 * elems
    rim = in_rows.shape[0] // 2
    size = lax.axis_size("valve")
    me = lax.axis_index("valve")
    up, down = lax.rem(me + 1, size), lax.rem(me + size - 1, size)
    barrier = pltpu.get_barrier_semaphore()
    for peer in (up, down):
        pl.semaphore_signal(barrier, inc=1, device_id={"valve": peer}, device_id_type=MESH)
    ext = ext_ref[...]
    speeds = by_face(speed_ref, tiles)
    for v in range(nvars):
        vals = dot(ext, split_rows(sol_ref[v]))
        for f in range(6):
            nat[f, 16 * v : 16 * v + 16, :] = vals[16 * f : 16 * f + 16]
    picked = jnp.zeros((2 * rim, 128), jnp.float32)
    slot = lax.broadcasted_iota(jnp.int32, (2 * rim, elems), 0) + faces_total
    for f in range(6):
        nat[f, 16 * nvars : 16 * nvars + 16, :] = speeds[f]
        nat[f, 16 * nvars + 16 :, :] = jnp.zeros((112 - 16 * nvars, elems), jnp.float32)
        rows = nat[f].T
        table_ref[f * elems : (f + 1) * elems, :] = rows
        onehot = (links_ref[f : f + 1, :] == slot).astype(jnp.float32).astype(jnp.bfloat16)
        hi, lo = halves(rows)
        picked = picked + dot(onehot, hi) + dot(onehot, lo)
    out_rows[...] = picked
    pl.semaphore_wait(barrier, 2)
    to_up = pltpu.make_async_remote_copy(
        src_ref=out_rows.at[rim:],
        dst_ref=in_rows.at[:rim],
        send_sem=send_sem.at[0],
        recv_sem=recv_sem.at[0],
        device_id={"valve": up},
        device_id_type=MESH,
    )
    to_down = pltpu.make_async_remote_copy(
        src_ref=out_rows.at[:rim],
        dst_ref=in_rows.at[rim:],
        send_sem=send_sem.at[1],
        recv_sem=recv_sem.at[1],
        device_id={"valve": down},
        device_id_type=MESH,
    )
    to_up.start()
    to_down.start()
    to_up.wait()
    to_down.wait()
    table_ref[faces_total:, :] = in_rows[...]


def face_table(solution, face_speed, face_link, extrapolate):
    elems = solution.shape[2]
    rim = elems // 16
    vmem = pl.BlockSpec(memory_space=pltpu.VMEM)
    return pl.pallas_call(
        table_kernel,
        out_shape=jax.ShapeDtypeStruct((6 * elems + 2 * rim, 128), jnp.float32),
        in_specs=[vmem] * 4,
        out_specs=vmem,
        scratch_shapes=[
            pltpu.VMEM((6, 128, elems), jnp.float32),
            pltpu.VMEM((elems // 128, 96, 128), jnp.float32),
            pltpu.VMEM((2 * rim, 128), jnp.float32),
            pltpu.VMEM((2 * rim, 128), jnp.float32),
            pltpu.SemaphoreType.DMA((2,)),
            pltpu.SemaphoreType.DMA((2,)),
        ],
        compiler_params=pltpu.CompilerParams(
            collective_id=0, has_side_effects=True, vmem_limit_bytes=VMEM_BYTES
        ),
        name="face_table",
    )(solution, face_speed, face_link, extrapolate)


def section_kernel(
    links_ref, table_ref, sol_ref, vel_ref, jac_ref, speed_ref, ops_ref, lift_ref,
    rate_ref, hi_ref, lo_ref, even, odd, jump, tiles,
):
    nvars, _, width = sol_ref.shape
    half = 128
    step = pl.program_id(0)
    last = pl.num_programs(0) * width - half
    ops = ops_ref[...]
    lift = lift_ref[...]

    def fetch(rows, f, u, start):
        rows[f, pl.ds(u, 1), :] = table_ref[links_ref[f, start + u]]

    @pl.when(step == 0)
    def _():
        def eight(i, carry):
            for f in range(6):
                for u in range(8):
                    fetch(even, f, pl.multiple_of(8 * i, 8) + u, 0)
            return carry

        lax.fori_loop(0, half // 8, eight, 0)

    def work(rows, span, coming, start):
        vel = vel_ref[:, span]
        jac = jac_ref[:, span]
        tiles[...] = speed_ref[:, span]
        sol = [sol_ref[v, :, span] for v in range(nvars)]
        own = [dot(ops, split_rows(sol[v])) for v in range(nvars)]
        for f in range(6):
            for u in range(half):
                fetch(coming, f, u, start)
            outer = rows[f].T
            speed = tiles[pl.ds(f, 16, stride=6), :]
            normal = 0.5 * (speed - outer[16 * nvars : 16 * nvars + 16])
            mean, diff = 0.5 * normal, 0.5 * jnp.abs(normal)
            for v in range(nvars):
                inner = own[v][16 * f : 16 * f + 16]
                other = outer[16 * v : 16 * v + 16]
                jump[v, 16 * f : 16 * f + 16, :] = (
                    mean * (inner + other) + diff * (inner - other) - speed * inner
                )
        for v in range(nvars):
            total = dot(lift, split_rows(jump[v]))
            for d in range(3):
                total = total + vel[d : d + 1] * own[v][96 + 64 * d : 160 + 64 * d]
            rate = -jac * total
            rate_ref[v, :, span] = rate
            hi, lo = halves(sol[v] + section_step * rate)
            hi_ref[64 * v : 64 * v + 64, span] = hi
            lo_ref[64 * v : 64 * v + 64, span] = lo

    base = step * width
    work(even, slice(0, half), odd, base + half)
    work(odd, slice(half, 2 * half), even, jnp.minimum(base + 2 * half, last))


def section(face_link, table, solution, velocity, inv_jacobian, face_speed, operators, lifting):
    nvars, points, elems = solution.shape
    width = 256
    whole = pl.BlockSpec(memory_space=pltpu.VMEM)
    block = lambda rows: pl.BlockSpec((rows, width), lambda i, links: (0, i))
    cube = pl.BlockSpec((nvars, points, width), lambda i, links: (0, 0, i))
    pieces = jax.ShapeDtypeStruct((nvars * points, elems), jnp.bfloat16)
    return pl.pallas_call(
        section_kernel,
        grid_spec=pltpu.PrefetchScalarGridSpec(
            num_scalar_prefetch=1,
            grid=(elems // width,),
            in_specs=[whole, cube, block(3), block(64), block(96), whole, whole],
            out_specs=[cube, block(nvars * points), block(nvars * points)],
            scratch_shapes=[
                pltpu.VMEM((6, 128, 128), jnp.float32),
                pltpu.VMEM((6, 128, 128), jnp.float32),
                pltpu.VMEM((nvars, 96, 128), jnp.float32),
                pltpu.VMEM((96, 128), jnp.float32),
            ],
        ),
        out_shape=[jax.ShapeDtypeStruct(solution.shape, jnp.float32), pieces, pieces],
        compiler_params=pltpu.CompilerParams(vmem_limit_bytes=VMEM_BYTES),
        name="section",
    )(face_link, table.reshape(-1, 1, 128), solution, velocity, inv_jacobian, face_speed, operators, lifting)


def one_hot(rows, index, dtype=jnp.int16):
    count = lax.broadcasted_iota(dtype, (rows, index.shape[1]), 0)
    return jnp.where(count == index.astype(dtype), jnp.bfloat16(1), jnp.bfloat16(0))


def receptor_kernel(buckets, nvars, hi_ref, lo_ref, donor_ref, coord_ref, owner_ref, out_ref, pieces, acc, seen):
    elems = hi_ref.shape[1]
    width = donor_ref.shape[1]
    part = 512
    tile = 256
    capacity = 16384 // buckets
    step = pl.program_id(0)
    rows = nvars * 64

    @pl.when(step == 0)
    def _():
        pieces[:rows, :] = hi_ref[...]
        pieces[rows:, :] = lo_ref[...]

    owner = owner_ref[...]
    named = (lax.broadcasted_iota(jnp.int32, (16, width), 0) == owner).astype(jnp.float32)
    upper = (
        lax.broadcasted_iota(jnp.int32, (tile, tile), 0)
        < lax.broadcasted_iota(jnp.int32, (tile, tile), 1)
    ).astype(jnp.float32).astype(jnp.bfloat16)
    tiles = [named[:, t : t + tile] for t in range(0, width, tile)]
    before = dot(jnp.concatenate(tiles, axis=0).astype(jnp.bfloat16), upper)
    carry = jnp.where(step == 0, 0.0, seen[...])[:, 0:1]
    ranks = []
    for t, own in enumerate(tiles):
        ranks.append(jnp.sum(own * (before[16 * t : 16 * t + 16] + carry), axis=0, keepdims=True))
        carry = carry + jnp.sum(own, axis=1, keepdims=True)
    seen[...] = jnp.broadcast_to(carry, seen.shape)
    place = owner * capacity + jnp.concatenate(ranks, axis=1).astype(jnp.int32)
    in_row = one_hot(64, place // 256)
    in_lane = one_hot(256, lax.rem(place, 256))

    both_pieces = pieces[...]
    columns = []
    for start in range(0, width, part):
        span = slice(start, start + part)
        picked = dot(both_pieces, one_hot(elems, donor_ref[:, span]))
        lx = lagrange_at(coord_ref[0:1, span])
        ly = lagrange_at(coord_ref[1:2, span])
        lz = jnp.concatenate(lagrange_at(coord_ref[2:3, span]), axis=0)
        yz = jnp.concatenate([ly[j] * lz for j in range(4)], axis=0)
        weights = jnp.concatenate([lx[i] * yz for i in range(4)], axis=0)
        parts = []
        for v in range(nvars):
            both = picked[64 * v : 64 * v + 64] + picked[rows + 64 * v : rows + 64 * v + 64]
            value = jnp.sum(both * weights, axis=0, keepdims=True)
            for piece in halves(value):
                parts.append(in_row[:, span] * piece)
        columns.append(jnp.concatenate(parts, axis=0))
    spread = dot_nt(jnp.concatenate(columns, axis=1), in_lane)
    acc[...] = jnp.where(step == 0, 0.0, acc[...]) + spread

    @pl.when(step == pl.num_programs(0) - 1)
    def _():
        for v in range(nvars):
            both = acc[128 * v : 128 * v + 64, :] + acc[128 * v + 64 : 128 * v + 128, :]
            out_ref[pl.ds(v, 64, stride=2 * nvars), :] = both[:, :128]
            out_ref[pl.ds(nvars + v, 64, stride=2 * nvars), :] = both[:, 128:]


def receptor_slots(hi, lo, donors, coords, owners, buckets):
    rows, elems = hi.shape
    nvars = rows // 64
    receptors = donors.shape[1]
    width = 2048
    whole = pl.BlockSpec(memory_space=pltpu.VMEM)
    block = lambda count: pl.BlockSpec((count, width), lambda i: (0, i))
    return pl.pallas_call(
        functools.partial(receptor_kernel, buckets, nvars),
        grid=(receptors // width,),
        in_specs=[whole, whole, block(1), block(3), block(1)],
        out_specs=pl.BlockSpec((nvars * 128, 128), lambda i: (0, 0)),
        out_shape=jax.ShapeDtypeStruct((nvars * 128, 128), jnp.float32),
        scratch_shapes=[
            pltpu.VMEM((2 * rows, elems), jnp.bfloat16),
            pltpu.VMEM((128 * nvars, 256), jnp.float32),
            pltpu.VMEM((16, 128), jnp.float32),
        ],
        compiler_params=pltpu.CompilerParams(vmem_limit_bytes=VMEM_BYTES),
        name="receptor_slots",
    )(hi, lo, donors, coords, owners)


def exchange_kernel(buckets, nvars, send_ref, out_ref, held, send_sem, recv_sem):
    block = nvars * 128 // buckets
    me = lax.axis_index("bulk")
    barrier = pltpu.get_barrier_semaphore()
    peers = [lax.rem(me + k, buckets) for k in range(1, buckets)]
    for peer in peers:
        pl.semaphore_signal(barrier, inc=1, device_id={"bulk": peer}, device_id_type=MESH)
    pl.semaphore_wait(barrier, buckets - 1)
    mine = pl.ds(pl.multiple_of(me * block, 8), block)
    copies = []
    for k, peer in enumerate(peers):
        copy = pltpu.make_async_remote_copy(
            src_ref=send_ref.at[pl.ds(pl.multiple_of(peer * block, 8), block)],
            dst_ref=held.at[mine],
            send_sem=send_sem.at[k],
            recv_sem=recv_sem.at[k],
            device_id={"bulk": peer},
            device_id_type=MESH,
        )
        copy.start()
        copies.append(copy)
    held[mine, :] = send_ref[mine, :]
    for copy in copies:
        copy.wait()
    for j in range(128):
        out_ref[:, 128 * j : 128 * j + 128] = held[nvars * j : nvars * j + nvars, :]


def exchange(slots, nvars, buckets):
    vmem = pl.BlockSpec(memory_space=pltpu.VMEM)
    return pl.pallas_call(
        functools.partial(exchange_kernel, buckets, nvars),
        out_shape=jax.ShapeDtypeStruct((nvars, 16384), jnp.float32),
        in_specs=[vmem],
        out_specs=vmem,
        scratch_shapes=[
            pltpu.VMEM(slots.shape, jnp.float32),
            pltpu.SemaphoreType.DMA((buckets - 1,)),
            pltpu.SemaphoreType.DMA((buckets - 1,)),
        ],
        compiler_params=pltpu.CompilerParams(
            collective_id=1, has_side_effects=True, vmem_limit_bytes=VMEM_BYTES
        ),
        name="exchange",
    )(slots)


def on_device(
    solution, velocity, inv_jacobian, face_speed, face_link, donor_elem, ref_coords, owner_list
):
    extrapolate, derivative, lifting = tables()
    nvars = solution.shape[0]
    buckets = lax.axis_size("bulk")
    operators = np.concatenate([extrapolate, derivative.reshape(192, 64)], axis=0)
    table = face_table(solution, face_speed, face_link, split_columns(extrapolate))
    section_rate, hi, lo = section(
        face_link, table, solution, velocity, inv_jacobian, face_speed,
        split_columns(operators), split_columns(lifting),
    )
    slots = receptor_slots(
        hi, lo, donor_elem.reshape(1, -1), ref_coords, owner_list.reshape(1, -1), buckets
    )
    return (section_rate, exchange(slots, nvars, buckets))


def solution(mesh):
    placed = (
        P(None, None, ("valve", "bulk")),
        P(None, ("valve", "bulk")),
        P(None, ("valve", "bulk")),
        P(None, ("valve", "bulk")),
        P(None, ("valve", "bulk")),
        P(("valve", "bulk")),
        P(None, ("valve", "bulk")),
        P(("valve", "bulk"), None),
    )
    return jax.shard_map(
        on_device,
        mesh=mesh,
        in_specs=placed,
        out_specs=(P(None, None, ("valve", "bulk")), P(None, ("valve", "bulk"))),
        check_vma=False,
    )
```
